32 devices in a mesh: depth: 2 (over core), tiles: 16 (over z, y, x).
Axes of the slice: x: 2, y: 2, z: 4, core: 2. Of those that a mesh axis runs over, the one named last changes fastest.
Arguments:
- transmission: float32 [4, 2, 16, 256, 256], P('depth', None, 'tiles'), may hold values from -0.4 to 1.3
- illumination: float32 [2, 256, 256], replicated, may hold values from -6 to 6
- fresnel_taps: float32 [2, 31], replicated, may hold values from -1 to 1
- intensity: float32 [16, 2, 256, 256], P('tiles'), may hold values from 0 to 2
- offsets: int32 [16, 2, 2], P('tiles'), may hold values from 0 to 255, as said below
- counts: int32 [16], P('tiles'), may hold values from 0 to 2, as said below
Outputs:
- object_gradient: float32 [4, 2, 16, 256, 256], P('depth', None, 'tiles')
The draws below stay inside these ranges and needn't reach their ends.
Inputs may be any that keep to these rules, and one draw needn't show every extreme that they name: `offsets`: A tile in the last row of tiles has row offset 0 in every slot, and a tile in the last column of tiles has column offset 0 in every slot, so every patch lies inside the object. Slots j >= counts[t] of tile t are unused.
All inputs are finite; a program needn't handle non-finite values.
Results may differ from the reference program's by a relative error of at most 0.0003.
Values sent between devices are 32-bit elements; how exact they have to be, the bound alone decides.
A program may use at most 64 MiB of HBM per device.

```python
import math
import jax
import jax.numpy as jnp
from jax import lax

P_SIZE = 256
KT = 31
GX = 4
CAP = 2
S = 256
SLICES = 4
TILE_COUNT = 16


sample_total = 64


def draw_transmission(key, part):
    key_real = jax.random.fold_in(key, 11)
    key_imag = jax.random.fold_in(key, 12)
    shape_one = (SLICES, TILE_COUNT, S, S)
    real_part = jax.random.uniform(key_real, shape_one, jnp.float32, 0.65, 1.25)
    imag_part = jax.random.uniform(key_imag, shape_one, jnp.float32, -0.3, 0.3)
    return jnp.stack([real_part, imag_part], 1)


def draw_fresnel_taps(key, part):
    key_main = jax.random.fold_in(key, 41)
    key_fourth = jax.random.fold_in(key, 42)
    key_tilt = jax.random.fold_in(key, 43)
    strength = jax.random.uniform(key_main, (), jnp.float32, 2.0, 4.0)
    fourth = jax.random.uniform(key_fourth, (), jnp.float32, -0.5, 0.5)
    tilt = jax.random.uniform(key_tilt, (), jnp.float32, -0.5, 0.5)
    half_taps = KT // 2
    lag_values = (lax.broadcasted_iota(jnp.int32, (KT, sample_total), 0) - half_taps).astype(jnp.float32)
    theta = lax.broadcasted_iota(jnp.int32, (KT, sample_total), 1).astype(jnp.float32) * (2.0 * math.pi / sample_total)
    phase = strength * jnp.cos(theta) + fourth * jnp.cos(2.0 * theta) + tilt * jnp.sin(theta) + lag_values * theta
    taps_real = jnp.mean(jnp.cos(phase), axis=1)
    taps_imag = jnp.mean(jnp.sin(phase), axis=1)
    return jnp.stack([taps_real, taps_imag], 0)


def draw_offsets(key, part):
    key_row = jax.random.fold_in(key, 21)
    key_col = jax.random.fold_in(key, 22)
    tile_index = lax.broadcasted_iota(jnp.int32, (TILE_COUNT, CAP), 0)
    slot_index = lax.broadcasted_iota(jnp.int32, (TILE_COUNT, CAP), 1)
    row_offset = jax.random.randint(key_row, (TILE_COUNT, CAP), 0, S, dtype=jnp.int32)
    col_offset = jax.random.randint(key_col, (TILE_COUNT, CAP), 0, S, dtype=jnp.int32)
    first_slot = (tile_index == 0) & (slot_index == 0)
    row_offset = jnp.where(first_slot, S - 1, row_offset)
    col_offset = jnp.where(first_slot, S - 1, col_offset)
    row_offset = jnp.where(tile_index // GX < TILE_COUNT // GX - 1, row_offset, 0)
    col_offset = jnp.where(tile_index % GX < GX - 1, col_offset, 0)
    return jnp.stack([row_offset, col_offset], -1)


def draw_counts(key, part):
    key_base = jax.random.fold_in(key, 31)
    key_busy = jax.random.fold_in(key, 32)
    tile_index = lax.broadcasted_iota(jnp.int32, (TILE_COUNT,), 0)
    base_counts = jax.random.randint(key_base, (TILE_COUNT,), 0, CAP + 1, dtype=jnp.int32)
    busiest = jax.random.randint(key_busy, (), 0, TILE_COUNT, dtype=jnp.int32)
    emptiest = (busiest + 1) % TILE_COUNT
    base_counts = jnp.where(tile_index == busiest, CAP, base_counts)
    return jnp.where(tile_index == emptiest, 0, base_counts)


def level_of(stream_key, dims, cuts, low, largest):
    def one(dim, shards_of):
        heights = jax.random.uniform(jax.random.fold_in(jax.random.fold_in(stream_key, 6), dim), (shards_of,), jnp.float32, low / len(cuts), largest / len(cuts))
        return jnp.repeat(jnp.exp(heights), dims[dim] // shards_of).reshape((-1,) + (1,) * (len(dims) - dim - 1))

    gain = one(*cuts[0])
    for cut in cuts[1:]:
        gain = gain * one(*cut)
    return gain


def centred(key, dims, scale, bound, kind=jnp.bfloat16):
    return jnp.clip(scale * jax.random.normal(key, dims, jnp.float32), -bound, bound).astype(kind)


def setup_inputs(seed: int = 0) -> dict:
    keys = jax.random.split(jax.random.key(seed), 7)
    transmission = draw_transmission(jax.random.fold_in(keys[6], 71), 0)
    illumination = centred(keys[1], (2, P_SIZE, P_SIZE), 1.0, 6.0, jnp.float32)
    fresnel_taps = draw_fresnel_taps(jax.random.fold_in(keys[6], 71), 0)
    intensity = jnp.clip(2.0 * jax.random.uniform(keys[3], (TILE_COUNT, CAP, P_SIZE, P_SIZE), jnp.float32) ** level_of(keys[3], (TILE_COUNT, CAP, P_SIZE, P_SIZE), ((0, 16),), -0.2, 0.2), 0.0, 2.0)
    offsets = draw_offsets(jax.random.fold_in(keys[6], 71), 0)
    counts = draw_counts(jax.random.fold_in(keys[6], 71), 0)
    return dict(transmission=transmission, illumination=illumination, fresnel_taps=fresnel_taps, intensity=intensity, offsets=offsets, counts=counts)


def convolve(field_real, field_imag, fresnel_taps, axis_no):
    half_taps = fresnel_taps.shape[1] // 2
    extent = field_real.shape[axis_no]
    padding = [(0, 0), (0, 0)]
    padding[axis_no] = (half_taps, half_taps)
    padded_real = jnp.pad(field_real, padding)
    padded_imag = jnp.pad(field_imag, padding)
    result_real = jnp.zeros_like(field_real)
    result_imag = jnp.zeros_like(field_imag)
    for tap_index in range(fresnel_taps.shape[1]):
        moved_real = lax.slice_in_dim(padded_real, tap_index, tap_index + extent, axis=axis_no)
        moved_imag = lax.slice_in_dim(padded_imag, tap_index, tap_index + extent, axis=axis_no)
        tap_real = fresnel_taps[0, tap_index]
        tap_imag = fresnel_taps[1, tap_index]
        result_real = result_real + tap_real * moved_real - tap_imag * moved_imag
        result_imag = result_imag + tap_imag * moved_real + tap_real * moved_imag
    return (result_real, result_imag)

def patch_misfit(patches, illumination, fresnel_taps, measured, live_flag):
    wave_real = illumination[0]
    wave_imag = illumination[1]
    for slice_index in range(SLICES):
        object_real = patches[slice_index, 0]
        object_imag = patches[slice_index, 1]
        mixed_real = wave_real * object_real - wave_imag * object_imag
        mixed_imag = wave_real * object_imag + wave_imag * object_real
        half_real, half_imag = convolve(mixed_real, mixed_imag, fresnel_taps, 0)
        wave_real, wave_imag = convolve(half_real, half_imag, fresnel_taps, 1)
    spectrum = jnp.fft.fft2(wave_real + 1j * wave_imag, norm='ortho')
    power = jnp.real(spectrum) ** 2 + jnp.imag(spectrum) ** 2
    misfit = live_flag * (power - measured)
    return 0.5 * jnp.sum(misfit * misfit)

def assemble(tiled):
    tile_rows = TILE_COUNT // GX
    shaped = tiled.reshape(SLICES, 2, tile_rows, GX, S, S)
    shaped = jnp.transpose(shaped, (0, 1, 2, 4, 3, 5))
    return shaped.reshape(SLICES, 2, tile_rows * S, GX * S)

def disassemble(whole):
    tile_rows = TILE_COUNT // GX
    shaped = whole.reshape(SLICES, 2, tile_rows, S, GX, S)
    shaped = jnp.transpose(shaped, (0, 1, 2, 4, 3, 5))
    return shaped.reshape(SLICES, 2, TILE_COUNT, S, S)

def reference(transmission, illumination, fresnel_taps, intensity, offsets, counts):
    whole = assemble(transmission)
    flat_offsets = offsets.reshape(TILE_COUNT * CAP, 2).astype(jnp.int32)
    tile_ids = jnp.repeat(jnp.arange(TILE_COUNT, dtype=jnp.int32), CAP)
    slot_ids = jnp.tile(jnp.arange(CAP, dtype=jnp.int32), TILE_COUNT)
    live_all = (slot_ids < counts[tile_ids]).astype(whole.dtype)
    measured_all = intensity.reshape(TILE_COUNT * CAP, P_SIZE, P_SIZE)
    row_starts = (tile_ids // GX * S + flat_offsets[:, 0]).astype(jnp.int32)
    col_starts = (tile_ids % GX * S + flat_offsets[:, 1]).astype(jnp.int32)
    zero_index = jnp.zeros((), jnp.int32)

    def accumulate(gradient, item):
        row_start, col_start, measured, live_flag = item
        corner = (zero_index, zero_index, row_start, col_start)
        patches = lax.dynamic_slice(whole, corner, (SLICES, 2, P_SIZE, P_SIZE))
        loss, pullback = jax.vjp(lambda block: patch_misfit(block, illumination, fresnel_taps, measured, live_flag), patches)
        patch_gradient, = pullback(jnp.ones_like(loss))
        current = lax.dynamic_slice(gradient, corner, (SLICES, 2, P_SIZE, P_SIZE))
        return (lax.dynamic_update_slice(gradient, current + patch_gradient, corner), None)
    gradient, unused = lax.scan(accumulate, jnp.zeros_like(whole), (row_starts, col_starts, measured_all, live_all))
    return disassemble(gradient)
```

```python
import math

import jax
import jax.numpy as jnp
import numpy as np
from jax import lax
from jax.experimental import pallas as pl
from jax.experimental.pallas import tpu as pltpu
from jax.sharding import PartitionSpec as P

GX = 4
F32 = jnp.float32
BF16 = jnp.bfloat16


def shifted(block, axis, by):
    peers = lax.axis_size(axis)
    pairs = [(i, i + by) for i in range(peers) if 0 <= i + by < peers]
    return lax.ppermute(block, axis, pairs)


def swapped(block):
    return lax.ppermute(block, "depth", [(0, 1), (1, 0)])


def halves(value):
    high = value.astype(BF16)
    return high, (value - high.astype(F32)).astype(BF16)


def fourier_planes(side):
    index = np.arange(side)
    phase = (index[:, None] * index[None, :] % side) * (2.0 * math.pi / side)
    planes = np.stack([np.cos(phase), -np.sin(phase)]) / math.sqrt(side)
    return planes.astype(np.float32)


def put_left(table, real, imag, row, rows):
    side = real.shape[1]
    rh, rl = halves(real)
    ih, il = halves(imag)
    for at, (top, low) in enumerate(((rh, ih), (rh, ih), (rl, il), (-ih, rh), (-ih, rh), (-il, rl))):
        cols = slice(at * side, (at + 1) * side)
        table[pl.ds(row, rows), cols] = top
        table[pl.ds(row + side, rows), cols] = low


def put_right(table, real, imag, row, rows):
    side = real.shape[1]
    rh, rl = halves(real)
    ih, il = halves(imag)
    for at, (first, second) in enumerate(((rh, ih), (rl, il), (rh, ih), (-ih, rh), (-il, rl), (-ih, rh))):
        table[pl.ds(row + at * side, rows), 0:side] = first
        table[pl.ds(row + at * side, rows), side:] = second


def from_left(table, stack, real, imag):
    side = real.shape[0]
    rh, rl = halves(real)
    ih, il = halves(imag)
    for at, part in enumerate((rh, rl, rh, ih, il, ih)):
        stack[at * side:(at + 1) * side, :] = part
    both = jnp.dot(table[...], stack[...], preferred_element_type=F32)
    return both[:side], both[side:]


def from_right(table, line, real, imag):
    side = real.shape[0]
    rh, rl = halves(real)
    ih, il = halves(imag)
    for at, part in enumerate((rh, rh, rl, ih, ih, il)):
        line[:, at * side:(at + 1) * side] = part
    both = jnp.dot(line[...], table[...], preferred_element_type=F32)
    return both[:, :side], both[:, side:]


def wave_kernel(
    scalars, taps, mine, other, probe, measured, fourier, grad_mine, grad_other,
    left_f, left_b, right_f, right_b, four_l, four_r, saved, stack, line,
):
    side = probe.shape[-1]
    per = mine.shape[0]
    layers = 2 * per
    row_at, col_at, live, depth = scalars[0], scalars[1], scalars[2], scalars[3]
    tap_count = taps.shape[1]
    half = tap_count // 2
    rows = 16

    @pl.when(live == 0)
    def _():
        grad_mine[...] = jnp.zeros_like(grad_mine)
        grad_other[...] = jnp.zeros_like(grad_other)

    @pl.when(live != 0)
    def _():
        def tables(block, unused):
            row = pl.multiple_of(block * rows, rows)
            i = lax.broadcasted_iota(jnp.int32, (rows, side), 0) + row
            j = lax.broadcasted_iota(jnp.int32, (rows, side), 1)
            lag = j - i
            lag = jnp.where(lag > side // 2, lag - side, lag)
            lag = jnp.where(lag < -(side // 2), lag + side, lag)
            zero = jnp.zeros((rows, side), F32)
            fr, fi, br, bi = zero, zero, zero, zero
            for tap in range(tap_count):
                on = lag == tap - half
                back = tap_count - 1 - tap
                fr = jnp.where(on, taps[0, tap], fr)
                fi = jnp.where(on, taps[1, tap], fi)
                br = jnp.where(on, taps[0, back], br)
                bi = jnp.where(on, taps[1, back], bi)

            def inside(corner):
                ii = jnp.where(i < corner, i + side, i)
                jj = jnp.where(j < corner, j + side, j)
                return jj - ii == lag

            keep = inside(row_at)
            put_left(left_f, jnp.where(keep, fr, 0.0), jnp.where(keep, fi, 0.0), row, rows)
            put_left(left_b, jnp.where(keep, br, 0.0), jnp.where(keep, -bi, 0.0), row, rows)
            keep = inside(col_at)
            put_right(right_f, jnp.where(keep, br, 0.0), jnp.where(keep, bi, 0.0), row, rows)
            put_right(right_b, jnp.where(keep, fr, 0.0), jnp.where(keep, -fi, 0.0), row, rows)
            return unused

        lax.fori_loop(0, side // rows, tables, 0)
        put_left(four_l, fourier[0], fourier[1], 0, side)
        put_right(four_r, fourier[0], fourier[1], 0, side)

        def layer(k):
            here = depth == k // per
            return [jnp.where(here, mine[k % per, c], other[k % per, c]) for c in range(2)]

        for c in range(2):
            saved[0, c] = pltpu.roll(pltpu.roll(probe[c], row_at, 0), col_at, 1)
        for k in range(layers):
            wr, wi = saved[k, 0], saved[k, 1]
            o_r, o_i = layer(k)
            wr, wi = wr * o_r - wi * o_i, wr * o_i + wi * o_r
            wr, wi = from_left(left_f, stack, wr, wi)
            wr, wi = from_right(right_f, line, wr, wi)
            if k < layers - 1:
                saved[k + 1, 0] = wr
                saved[k + 1, 1] = wi
        wr, wi = from_left(four_l, stack, wr, wi)
        wr, wi = from_right(four_r, line, wr, wi)
        misfit = 2.0 * (wr * wr + wi * wi - measured[depth])
        put_left(four_l, fourier[0], -fourier[1], 0, side)
        put_right(four_r, fourier[0], -fourier[1], 0, side)
        gr, gi = misfit * wr, misfit * wi
        gr, gi = from_left(four_l, stack, gr, gi)
        gr, gi = from_right(four_r, line, gr, gi)
        for k in reversed(range(layers)):
            gr, gi = from_left(left_b, stack, gr, gi)
            gr, gi = from_right(right_b, line, gr, gi)
            wr, wi = saved[k, 0], saved[k, 1]
            pr, pi = wr * gr + wi * gi, wr * gi - wi * gr

            @pl.when(depth == k // per)
            def _():
                grad_mine[k % per, 0] = pr
                grad_mine[k % per, 1] = pi

            @pl.when(depth != k // per)
            def _():
                grad_other[k % per, 0] = pr
                grad_other[k % per, 1] = pi

            if k > 0:
                o_r, o_i = layer(k)
                gr, gi = o_r * gr + o_i * gi, o_r * gi - o_i * gr


def wave_call(scalars, taps, mine, other, probe, measured, fourier):
    side = probe.shape[-1]
    per = mine.shape[0]
    vmem = pl.BlockSpec(memory_space=pltpu.VMEM)
    smem = pl.BlockSpec(memory_space=pltpu.SMEM)
    out = jax.ShapeDtypeStruct(mine.shape, F32)
    tall = pltpu.VMEM((6 * side, 2 * side), BF16)
    wide = pltpu.VMEM((2 * side, 6 * side), BF16)
    return pl.pallas_call(
        wave_kernel,
        out_shape=(out, out),
        in_specs=[smem, smem] + [vmem] * 5,
        out_specs=(vmem, vmem),
        scratch_shapes=[
            wide, wide, tall, tall, wide, tall,
            pltpu.VMEM((2 * per, 2, side, side), F32),
            pltpu.VMEM((6 * side, side), BF16),
            pltpu.VMEM((side, 6 * side), BF16),
        ],
        compiler_params=pltpu.CompilerParams(vmem_limit_bytes=44 * 1024 * 1024),
        name="wave",
    )(scalars, taps, mine, other, probe, measured, fourier)


def local(transmission, illumination, fresnel_taps, intensity, offsets, counts):
    own = transmission[:, :, 0]
    side = own.shape[-1]
    corners = offsets[0]
    depth = lax.axis_index("depth")
    right = shifted(own, "tiles", -1)
    lower = shifted(own, "tiles", -GX)
    diag = shifted(own, "tiles", -GX - 1)
    i = lax.broadcasted_iota(jnp.int32, (side, side), 0)
    j = lax.broadcasted_iota(jnp.int32, (side, side), 1)

    def masks(slot):
        return i >= corners[slot, 0], j >= corners[slot, 1]

    def mosaic(slot):
        below, past = masks(slot)
        return jnp.where(below, jnp.where(past, own, right), jnp.where(past, lower, diag))

    mine = mosaic(depth)
    other = swapped(mosaic(1 - depth))
    live = (depth < counts[0]).astype(jnp.int32)
    scalars = jnp.stack([corners[depth, 0], corners[depth, 1], live, depth.astype(jnp.int32)])
    grad_mine, grad_other = wave_call(
        scalars, fresnel_taps, mine, other, illumination, intensity[0], jnp.asarray(fourier_planes(side))
    )
    grad_swap = swapped(grad_other)
    first, second = masks(depth), masks(1 - depth)

    def part(down, across):
        def one(mask, grad):
            keep = (mask[0] if down else ~mask[0]) & (mask[1] if across else ~mask[1])
            return jnp.where(keep, grad, 0.0)

        return one(first, grad_mine) + one(second, grad_swap)

    from_diag = shifted(part(False, False), "tiles", GX + 1)
    from_lower = shifted(part(False, True), "tiles", GX)
    from_right = shifted(part(True, False), "tiles", 1)
    total = part(True, True) + from_right + from_lower + from_diag
    return total[:, :, None]


def solution(mesh):
    placed = (
        P("depth", None, "tiles", None, None),
        P(),
        P(),
        P("tiles", None, None, None),
        P("tiles", None, None),
        P("tiles"),
    )
    return jax.shard_map(
        local,
        mesh=mesh,
        in_specs=placed,
        out_specs=P("depth", None, "tiles", None, None),
        check_vma=False,
    )
```

```python
import math

import jax
import jax.numpy as jnp
import numpy as np
from jax import lax
from jax.experimental import pallas as pl
from jax.experimental.pallas import tpu as pltpu
from jax.sharding import PartitionSpec as P

GX = 4
F32 = jnp.float32
BF16 = jnp.bfloat16


def shifted(block, rows, cols):
    peers = lax.axis_size("tiles")
    pairs = [
        (i, i + rows * GX + cols)
        for i in range(peers)
        if 0 <= i // GX + rows < peers // GX and 0 <= i % GX + cols < GX
    ]
    return lax.ppermute(block, "tiles", pairs)


def swapped(block):
    return lax.ppermute(block, "depth", [(0, 1), (1, 0)])


def halves(value):
    high = value.astype(BF16)
    return high, (value - high.astype(F32)).astype(BF16)


def fourier_planes(side):
    index = np.arange(side)
    phase = (index[:, None] * index[None, :] % side) * (2.0 * math.pi / side)
    planes = np.stack([np.cos(phase), -np.sin(phase)]) / math.sqrt(side)
    return planes.astype(np.float32)


def put_left(table, real, imag, row, rows):
    side = real.shape[1]
    rh, rl = halves(real)
    ih, il = halves(imag)
    for at, (top, low) in enumerate(((rh, ih), (rh, ih), (rl, il), (-ih, rh), (-ih, rh), (-il, rl))):
        cols = slice(at * side, (at + 1) * side)
        table[pl.ds(row, rows), cols] = top
        table[pl.ds(row + side, rows), cols] = low


def put_right(table, real, imag, row, rows):
    side = real.shape[1]
    rh, rl = halves(real)
    ih, il = halves(imag)
    for at, (first, second) in enumerate(((rh, ih), (rl, il), (rh, ih), (-ih, rh), (-il, rl), (-ih, rh))):
        table[pl.ds(row + at * side, rows), 0:side] = first
        table[pl.ds(row + at * side, rows), side:] = second


def from_left(table, stack, real, imag):
    side = real.shape[0]
    rh, rl = halves(real)
    ih, il = halves(imag)
    for at, part in enumerate((rh, rl, rh, ih, il, ih)):
        stack[at * side:(at + 1) * side, :] = part
    both = jnp.dot(table[...], stack[...], preferred_element_type=F32)
    return both[:side], both[side:]


def from_right(table, line, real, imag):
    side = real.shape[0]
    rh, rl = halves(real)
    ih, il = halves(imag)
    for at, part in enumerate((rh, rh, rl, ih, ih, il)):
        line[:, at * side:(at + 1) * side] = part
    both = jnp.dot(line[...], table[...], preferred_element_type=F32)
    return both[:, :side], both[:, side:]


def wave_kernel(
    scalars, taps, mine, other, probe, measured, fourier, grad_mine, grad_other,
    left_f, left_b, right_f, right_b, four_l, four_r, saved, stack, line,
):
    side = probe.shape[-1]
    per = mine.shape[0]
    layers = 2 * per
    row_at, col_at, live, depth = scalars[0], scalars[1], scalars[2], scalars[3]
    tap_count = taps.shape[1]
    half = tap_count // 2
    rows = 16

    @pl.when(live == 0)
    def _():
        grad_mine[...] = jnp.zeros_like(grad_mine)
        grad_other[...] = jnp.zeros_like(grad_other)

    @pl.when(live != 0)
    def _():
        def tables(block, unused):
            row = pl.multiple_of(block * rows, rows)
            i = lax.broadcasted_iota(jnp.int32, (rows, side), 0) + row
            j = lax.broadcasted_iota(jnp.int32, (rows, side), 1)
            lag = j - i
            lag = jnp.where(lag > side // 2, lag - side, lag)
            lag = jnp.where(lag < -(side // 2), lag + side, lag)
            zero = jnp.zeros((rows, side), F32)
            fr, fi, br, bi = zero, zero, zero, zero
            for tap in range(tap_count):
                on = lag == tap - half
                back = tap_count - 1 - tap
                fr = jnp.where(on, taps[0, tap], fr)
                fi = jnp.where(on, taps[1, tap], fi)
                br = jnp.where(on, taps[0, back], br)
                bi = jnp.where(on, taps[1, back], bi)

            def inside(corner):
                ii = jnp.where(i < corner, i + side, i)
                jj = jnp.where(j < corner, j + side, j)
                return jj - ii == lag

            keep = inside(row_at)
            put_left(left_f, jnp.where(keep, fr, 0.0), jnp.where(keep, fi, 0.0), row, rows)
            put_left(left_b, jnp.where(keep, br, 0.0), jnp.where(keep, -bi, 0.0), row, rows)
            keep = inside(col_at)
            put_right(right_f, jnp.where(keep, br, 0.0), jnp.where(keep, bi, 0.0), row, rows)
            put_right(right_b, jnp.where(keep, fr, 0.0), jnp.where(keep, -fi, 0.0), row, rows)
            return unused

        lax.fori_loop(0, side // rows, tables, 0)
        put_left(four_l, fourier[0], fourier[1], 0, side)
        put_right(four_r, fourier[0], fourier[1], 0, side)

        def layer(k):
            here = depth == k // per
            return [jnp.where(here, mine[k % per, c], other[k % per, c]) for c in range(2)]

        for c in range(2):
            saved[0, c] = pltpu.roll(pltpu.roll(probe[c], row_at, 0), col_at, 1)
        for k in range(layers):
            wr, wi = saved[k, 0], saved[k, 1]
            o_r, o_i = layer(k)
            wr, wi = wr * o_r - wi * o_i, wr * o_i + wi * o_r
            wr, wi = from_left(left_f, stack, wr, wi)
            wr, wi = from_right(right_f, line, wr, wi)
            if k < layers - 1:
                saved[k + 1, 0] = wr
                saved[k + 1, 1] = wi
        wr, wi = from_left(four_l, stack, wr, wi)
        wr, wi = from_right(four_r, line, wr, wi)
        misfit = 2.0 * (wr * wr + wi * wi - measured[depth])
        put_left(four_l, fourier[0], -fourier[1], 0, side)
        put_right(four_r, fourier[0], -fourier[1], 0, side)
        gr, gi = misfit * wr, misfit * wi
        gr, gi = from_left(four_l, stack, gr, gi)
        gr, gi = from_right(four_r, line, gr, gi)
        for k in reversed(range(layers)):
            gr, gi = from_left(left_b, stack, gr, gi)
            gr, gi = from_right(right_b, line, gr, gi)
            wr, wi = saved[k, 0], saved[k, 1]
            pr, pi = wr * gr + wi * gi, wr * gi - wi * gr

            @pl.when(depth == k // per)
            def _():
                grad_mine[k % per, 0] = pr
                grad_mine[k % per, 1] = pi

            @pl.when(depth != k // per)
            def _():
                grad_other[k % per, 0] = pr
                grad_other[k % per, 1] = pi

            if k > 0:
                o_r, o_i = layer(k)
                gr, gi = o_r * gr + o_i * gi, o_r * gi - o_i * gr


def wave_call(scalars, taps, mine, other, probe, measured, fourier):
    side = probe.shape[-1]
    per = mine.shape[0]
    vmem = pl.BlockSpec(memory_space=pltpu.VMEM)
    smem = pl.BlockSpec(memory_space=pltpu.SMEM)
    out = jax.ShapeDtypeStruct(mine.shape, F32)
    tall = pltpu.VMEM((6 * side, 2 * side), BF16)
    wide = pltpu.VMEM((2 * side, 6 * side), BF16)
    return pl.pallas_call(
        wave_kernel,
        out_shape=(out, out),
        in_specs=[smem, smem] + [vmem] * 5,
        out_specs=(vmem, vmem),
        scratch_shapes=[
            wide, wide, tall, tall, wide, tall,
            pltpu.VMEM((2 * per, 2, side, side), F32),
            pltpu.VMEM((6 * side, side), BF16),
            pltpu.VMEM((side, 6 * side), BF16),
        ],
        compiler_params=pltpu.CompilerParams(vmem_limit_bytes=44 * 1024 * 1024),
        name="wave",
    )(scalars, taps, mine, other, probe, measured, fourier)


def local(transmission, illumination, fresnel_taps, intensity, offsets, counts):
    own = transmission[:, :, 0]
    side = own.shape[-1]
    corners = offsets[0]
    depth = lax.axis_index("depth")
    right = shifted(own, 0, -1)
    lower = shifted(own, -1, 0)
    diag = shifted(own, -1, -1)
    i = lax.broadcasted_iota(jnp.int32, (side, side), 0)
    j = lax.broadcasted_iota(jnp.int32, (side, side), 1)

    def masks(slot):
        return i >= corners[slot, 0], j >= corners[slot, 1]

    def mosaic(slot):
        below, past = masks(slot)
        return jnp.where(below, jnp.where(past, own, right), jnp.where(past, lower, diag))

    mine = mosaic(depth)
    other = swapped(mosaic(1 - depth))
    live = (depth < counts[0]).astype(jnp.int32)
    scalars = jnp.stack([corners[depth, 0], corners[depth, 1], live, depth.astype(jnp.int32)])
    grad_mine, grad_other = wave_call(
        scalars, fresnel_taps, mine, other, illumination, intensity[0], jnp.asarray(fourier_planes(side))
    )
    grad_swap = swapped(grad_other)
    first, second = masks(depth), masks(1 - depth)

    def part(down, across):
        def one(mask, grad):
            keep = (mask[0] if down else ~mask[0]) & (mask[1] if across else ~mask[1])
            return jnp.where(keep, grad, 0.0)

        return one(first, grad_mine) + one(second, grad_swap)

    from_diag = shifted(part(False, False), 1, 1)
    from_lower = shifted(part(False, True), 1, 0)
    from_right = shifted(part(True, False), 0, 1)
    total = part(True, True) + from_right + from_lower + from_diag
    return total[:, :, None]


def solution(mesh):
    placed = (
        P("depth", None, "tiles", None, None),
        P(),
        P(),
        P("tiles", None, None, None),
        P("tiles", None, None),
        P("tiles"),
    )
    return jax.shard_map(
        local,
        mesh=mesh,
        in_specs=placed,
        out_specs=P("depth", None, "tiles", None, None),
        check_vma=False,
    )
```

```python
import math

import jax
import jax.numpy as jnp
import numpy as np
from jax import lax
from jax.experimental import pallas as pl
from jax.experimental.pallas import tpu as pltpu
from jax.sharding import PartitionSpec as P

GX = 4
F32 = jnp.float32
BF16 = jnp.bfloat16


def shifted(block, rows, cols):
    peers = lax.axis_size("tiles")
    pairs = [
        (i, i + rows * GX + cols)
        for i in range(peers)
        if 0 <= i // GX + rows < peers // GX and 0 <= i % GX + cols < GX
    ]
    return lax.ppermute(block, "tiles", pairs)


def swapped(block):
    return lax.ppermute(block, "depth", [(0, 1), (1, 0)])


def halves(value):
    high = value.astype(BF16)
    return high, (value - high.astype(F32)).astype(BF16)


def fourier_planes(side):
    index = np.arange(side)
    phase = (index[:, None] * index[None, :] % side) * (2.0 * math.pi / side)
    planes = np.stack([np.cos(phase), -np.sin(phase)]) / math.sqrt(side)
    return planes.astype(np.float32)


def put_left(table, real, imag, row, rows):
    side = real.shape[1]
    rh, rl = halves(real)
    ih, il = halves(imag)
    for at, (top, low) in enumerate(((rh, ih), (rh, ih), (rl, il), (-ih, rh), (-ih, rh), (-il, rl))):
        cols = slice(at * side, (at + 1) * side)
        table[pl.ds(row, rows), cols] = top
        table[pl.ds(row + side, rows), cols] = low


def put_right(table, real, imag, row, rows):
    side = real.shape[1]
    rh, rl = halves(real)
    ih, il = halves(imag)
    for at, (first, second) in enumerate(((rh, ih), (rl, il), (rh, ih), (-ih, rh), (-il, rl), (-ih, rh))):
        table[pl.ds(row + at * side, rows), 0:side] = first
        table[pl.ds(row + at * side, rows), side:] = second


def from_left(table, stack, real, imag):
    side = real.shape[0]
    rh, rl = halves(real)
    ih, il = halves(imag)
    for at, part in enumerate((rh, rl, rh, ih, il, ih)):
        stack[at * side:(at + 1) * side, :] = part
    both = jnp.dot(table[...], stack[...], preferred_element_type=F32)
    return both[:side], both[side:]


def from_right(table, line, real, imag):
    side = real.shape[0]
    rh, rl = halves(real)
    ih, il = halves(imag)
    for at, part in enumerate((rh, rh, rl, ih, ih, il)):
        line[:, at * side:(at + 1) * side] = part
    both = jnp.dot(line[...], table[...], preferred_element_type=F32)
    return both[:, :side], both[:, side:]


def table_kernel(
    scalars, taps, probe, fourier,
    left_f, left_b, right_f, right_b, far_lf, far_lb, far_rf, far_rb, rolled,
    four_l, four_r, band, stack, line,
):
    side = probe.shape[-1]
    row_at, col_at = scalars[0], scalars[1]
    tap_count = taps.shape[1]
    half = tap_count // 2
    rows = 16
    for c in range(2):
        rolled[c] = pltpu.roll(pltpu.roll(probe[c], row_at, 0), col_at, 1)

    def tables(block, unused):
        row = pl.multiple_of(block * rows, rows)
        i = lax.broadcasted_iota(jnp.int32, (rows, side), 0) + row
        j = lax.broadcasted_iota(jnp.int32, (rows, side), 1)
        lag = j - i
        lag = jnp.where(lag > side // 2, lag - side, lag)
        lag = jnp.where(lag < -(side // 2), lag + side, lag)
        zero = jnp.zeros((rows, side), F32)
        fr, fi, br, bi = zero, zero, zero, zero
        for tap in range(tap_count):
            on = lag == tap - half
            back = tap_count - 1 - tap
            fr = jnp.where(on, taps[0, tap], fr)
            fi = jnp.where(on, taps[1, tap], fi)
            br = jnp.where(on, taps[0, back], br)
            bi = jnp.where(on, taps[1, back], bi)

        def inside(corner):
            ii = jnp.where(i < corner, i + side, i)
            jj = jnp.where(j < corner, j + side, j)
            return jj - ii == lag

        keep = inside(row_at)
        real, imag = jnp.where(keep, fr, 0.0), jnp.where(keep, fi, 0.0)
        band[0, pl.ds(row, rows), :] = real
        band[1, pl.ds(row, rows), :] = imag
        put_left(left_f, real, imag, row, rows)
        put_left(left_b, jnp.where(keep, br, 0.0), jnp.where(keep, -bi, 0.0), row, rows)
        keep = inside(col_at)
        real, imag = jnp.where(keep, br, 0.0), jnp.where(keep, bi, 0.0)
        band[2, pl.ds(row, rows), :] = real
        band[3, pl.ds(row, rows), :] = imag
        put_right(right_f, real, imag, row, rows)
        put_right(right_b, jnp.where(keep, fr, 0.0), jnp.where(keep, -fi, 0.0), row, rows)
        return unused

    lax.fori_loop(0, side // rows, tables, 0)
    put_left(four_l, fourier[0], fourier[1], 0, side)
    put_right(four_r, fourier[0], fourier[1], 0, side)
    real, imag = from_left(four_l, stack, band[0], band[1])
    put_left(far_lf, real, imag, 0, side)
    put_left(far_lb, real.T, -imag.T, 0, side)
    real, imag = from_right(four_r, line, band[2], band[3])
    put_right(far_rf, real, imag, 0, side)
    put_right(far_rb, real.T, -imag.T, 0, side)


def wave_kernel(
    scalars, mine, other, probe, measured,
    left_f, left_b, right_f, right_b, far_lf, far_lb, far_rf, far_rb,
    grad_mine, grad_other, saved, stack, line,
):
    per = mine.shape[0]
    layers = 2 * per
    live, depth = scalars[2], scalars[3]

    @pl.when(live == 0)
    def _():
        grad_mine[...] = jnp.zeros_like(grad_mine)
        grad_other[...] = jnp.zeros_like(grad_other)

    @pl.when(live != 0)
    def _():
        def layer(k):
            here = depth == k // per
            return [jnp.where(here, mine[k % per, c], other[k % per, c]) for c in range(2)]

        wr, wi = probe[0], probe[1]
        for k in range(layers):
            last = k == layers - 1
            o_r, o_i = layer(k)
            wr, wi = wr * o_r - wi * o_i, wr * o_i + wi * o_r
            wr, wi = from_left(far_lf if last else left_f, stack, wr, wi)
            wr, wi = from_right(far_rf if last else right_f, line, wr, wi)
            if not last:
                saved[k, 0] = wr
                saved[k, 1] = wi
        misfit = 2.0 * (wr * wr + wi * wi - measured[depth])
        gr, gi = misfit * wr, misfit * wi
        for k in reversed(range(layers)):
            last = k == layers - 1
            gr, gi = from_left(far_lb if last else left_b, stack, gr, gi)
            gr, gi = from_right(far_rb if last else right_b, line, gr, gi)
            wave = saved.at[k - 1] if k > 0 else probe
            wr, wi = wave[0], wave[1]
            pr, pi = wr * gr + wi * gi, wr * gi - wi * gr

            @pl.when(depth == k // per)
            def _():
                grad_mine[k % per, 0] = pr
                grad_mine[k % per, 1] = pi

            @pl.when(depth != k // per)
            def _():
                grad_other[k % per, 0] = pr
                grad_other[k % per, 1] = pi

            if k > 0:
                o_r, o_i = layer(k)
                gr, gi = o_r * gr + o_i * gi, o_r * gi - o_i * gr


def wave_tables(scalars, taps, probe, fourier):
    side = probe.shape[-1]
    vmem = pl.BlockSpec(memory_space=pltpu.VMEM)
    smem = pl.BlockSpec(memory_space=pltpu.SMEM)
    tall = jax.ShapeDtypeStruct((6 * side, 2 * side), BF16)
    wide = jax.ShapeDtypeStruct((2 * side, 6 * side), BF16)
    return pl.pallas_call(
        table_kernel,
        out_shape=(wide, wide, tall, tall, wide, wide, tall, tall, jax.ShapeDtypeStruct(probe.shape, F32)),
        in_specs=[smem, smem, vmem, vmem],
        out_specs=(vmem,) * 9,
        scratch_shapes=[
            pltpu.VMEM(wide.shape, BF16),
            pltpu.VMEM(tall.shape, BF16),
            pltpu.VMEM((4, side, side), F32),
            pltpu.VMEM((6 * side, side), BF16),
            pltpu.VMEM((side, 6 * side), BF16),
        ],
        cost_estimate=pl.CostEstimate(flops=10**10, bytes_accessed=30 * 10**6, transcendentals=0),
        compiler_params=pltpu.CompilerParams(vmem_limit_bytes=36 * 1024 * 1024),
        name="tables",
    )(scalars, taps, probe, fourier)


def wave_call(scalars, mine, other, probe, measured, tables):
    side = probe.shape[-1]
    per = mine.shape[0]
    vmem = pl.BlockSpec(memory_space=pltpu.VMEM)
    smem = pl.BlockSpec(memory_space=pltpu.SMEM)
    out = jax.ShapeDtypeStruct(mine.shape, F32)
    return pl.pallas_call(
        wave_kernel,
        out_shape=(out, out),
        in_specs=[smem] + [vmem] * 12,
        out_specs=(vmem, vmem),
        scratch_shapes=[
            pltpu.VMEM((2 * per - 1, 2, side, side), F32),
            pltpu.VMEM((6 * side, side), BF16),
            pltpu.VMEM((side, 6 * side), BF16),
        ],
        compiler_params=pltpu.CompilerParams(vmem_limit_bytes=40 * 1024 * 1024),
        name="wave",
    )(scalars, mine, other, probe, measured, *tables)


def local(transmission, illumination, fresnel_taps, intensity, offsets, counts):
    own = transmission[:, :, 0]
    side = own.shape[-1]
    corners = offsets[0]
    depth = lax.axis_index("depth")
    right = shifted(own, 0, -1)
    lower = shifted(own, -1, 0)
    diag = shifted(own, -1, -1)
    i = lax.broadcasted_iota(jnp.int32, (side, side), 0)
    j = lax.broadcasted_iota(jnp.int32, (side, side), 1)

    def masks(slot):
        return i >= corners[slot, 0], j >= corners[slot, 1]

    def mosaic(slot):
        below, past = masks(slot)
        return jnp.where(below, jnp.where(past, own, right), jnp.where(past, lower, diag))

    live = (depth < counts[0]).astype(jnp.int32)
    scalars = jnp.stack([corners[depth, 0], corners[depth, 1], live, depth.astype(jnp.int32)])
    *tables, probe = wave_tables(scalars, fresnel_taps, illumination, jnp.asarray(fourier_planes(side)))
    right, lower, diag, probe, tables = lax.optimization_barrier((right, lower, diag, probe, tables))
    other = swapped(mosaic(1 - depth))
    mine = mosaic(depth)
    grad_mine, grad_other = wave_call(scalars, mine, other, probe, intensity[0], tables)
    grad_swap = swapped(grad_other)
    first, second = masks(depth), masks(1 - depth)

    def part(down, across):
        def one(mask, grad):
            keep = (mask[0] if down else ~mask[0]) & (mask[1] if across else ~mask[1])
            return jnp.where(keep, grad, 0.0)

        return one(first, grad_mine) + one(second, grad_swap)

    from_diag = shifted(part(False, False), 1, 1)
    from_lower = shifted(part(False, True), 1, 0)
    from_right = shifted(part(True, False), 0, 1)
    total = part(True, True) + from_right + from_lower + from_diag
    return total[:, :, None]


def solution(mesh):
    placed = (
        P("depth", None, "tiles", None, None),
        P(),
        P(),
        P("tiles", None, None, None),
        P("tiles", None, None),
        P("tiles"),
    )
    return jax.shard_map(
        local,
        mesh=mesh,
        in_specs=placed,
        out_specs=P("depth", None, "tiles", None, None),
        check_vma=False,
    )
```
